32 devices in a mesh: parts: 2 (over y), tile: 16 (over z, x, core).
Axes of the slice: x: 2, y: 2, z: 4, core: 2. Of those that a mesh axis runs over, the one named last changes fastest.
Arguments:
- density: bfloat16 [512, 256], P(('parts', 'tile')), parts along dimension 0, may hold values from -6 to 6
- three_center: bfloat16 [96, 32, 256, 128], P(('parts', 'tile')), parts along dimension 0, may hold values from -0.125 to 0.125
- metric: float32 [96, 128, 128], P(('parts', 'tile')), parts along dimension 0, may hold values from -1 to 2
- fetch_owner: int32 [11264, 1], P(('parts', 'tile')), parts along dimension 0, may hold values from 0 to 15; in each aligned block of 352 rows (0 to 351, 352 to 703, ...) at most 35 rows name the same one
- fetch_slot: int32 [11264], P(('parts', 'tile')), parts along dimension 0, may hold values from 0 to 15
- basis_value: bfloat16 [128, 32, 16, 128], P(('parts', 'tile')), parts along dimension 0, may hold values from -1 to 1
- basis_gradient: bfloat16 [128, 32, 3, 16, 128], P(('parts', 'tile')), parts along dimension 0, may hold values from -4 to 4
- pair_slot: int32 [128, 64, 2], P(('parts', 'tile')), parts along dimension 0, may hold values from 0 to 31
- base_density: float32 [128, 128], P(('parts', 'tile')), parts along dimension 0, may hold values from 0.3 to 3
- base_kinetic: float32 [128, 128], P(('parts', 'tile')), parts along dimension 0, may hold values from 4 to 40
- grid_weight: float32 [128, 128], P(('parts', 'tile')), parts along dimension 0, may hold values from 1 to 4
Outputs:
- coulomb: float32 [512, 256], P(('parts', 'tile')), parts along dimension 0
- exchange_corr: float32 [512, 256], P(('parts', 'tile')), parts along dimension 0
The draws below stay inside these ranges and needn't reach their ends.
There are 2 independent parts, one for each index of `parts`. The reference program is written for one: setup_inputs(seed, part) draws one part's arguments, and reference() takes and returns one part's arrays. A program takes and returns all parts, laid end to end along the dimension named above; each array names one. Nothing has to cross between parts.
Inputs may be any that keep to these rules, and one draw needn't show every extreme that they name: `fetch_owner`: in each of the 16 lists of 352 references, no owner is named more than 35 times, and in some list one owner is named exactly 35 times.
All inputs are finite; a program needn't handle non-finite values.
Results may differ from the reference program's by a relative error of at most 0.0049.
Values may be sent and summed in bfloat16 or wider, within the bound.
A program may use at most 64 MiB of HBM per device.

```python
import math
import jax
import jax.numpy as jnp
import numpy as np
from jax import lax

TB = 16
PT = 256
AB = 128
AUXB_DEV = 3
LJ = 32
TILE_DEV = 16
G = 128
KB = 32
LX = 64
NAUXB = 48
NTILE = 256
NBATCH = 64
REQ = 352
CAP = 35
N_TILE = 16


def draw_metric(key, part):
    key = jax.random.fold_in(key, 7)
    key_diag, key_noise = jax.random.split(key)
    diagonal = jax.random.uniform(key_diag, (NAUXB, AB), jnp.float32, 1.0, 2.0)
    noise = jax.random.normal(key_noise, (NAUXB, AB, AB), jnp.float32)
    symmetric = (noise + jnp.swapaxes(noise, 1, 2)) * (0.4 / math.sqrt(2.0 * AB))
    identity = jnp.eye(AB, dtype=jnp.float32)
    return symmetric * (1.0 - identity)[None] + identity[None] * diagonal[:, :, None]


def plant(result, own_key, low, largest):
    longest = result.shape.index(max(result.shape))
    spots = []
    for shift in (0, 1):
        where = [jax.random.randint(jax.random.fold_in(own_key, axis), (), 0, length) for axis, length in enumerate(result.shape)]
        where[longest] = (where[longest] + shift) % result.shape[longest]
        spots.append(tuple(where))
    return result.at[spots[0]].set(low).at[spots[1]].set(largest)


def shard_levels(key, shape, cuts, low, top_value):
    factor_of = 1.0
    for dim, blocks in cuts:
        steps = jax.random.uniform(jax.random.fold_in(jax.random.fold_in(key, 6), dim), (blocks,), jnp.float32, low / len(cuts), top_value / len(cuts))
        factor_of = factor_of * jnp.repeat(jnp.exp(steps), shape[dim] // blocks).reshape((-1,) + (1,) * (len(shape) - 1 - dim))
    return factor_of


def assign_block(stream_key, own, number, rows, number_of, top, limit, slope):
    order = jax.random.permutation(stream_key, number_of)
    packed, ordinary = load_shares(number_of, rows * top, limit, slope, True), load_shares(number_of, rows * top, limit, slope, False)
    places = jnp.arange(number_of)

    def named(tallies, rotation):
        used = int((tallies > 0).sum())
        fixed = max(1, used // 4)
        passed = fixed + (places - fixed + rotation * (used - fixed)) % max(1, number_of - fixed)
        return jnp.zeros((number_of,), jnp.int32).at[order[jnp.where(places < fixed, places, passed)]].set(jnp.asarray(tallies, jnp.int32))

    tallies = jnp.where(number % 4 == 0, named(packed, number // 4), named(ordinary, number - number // 4 - 1))
    mixed = jax.random.permutation(jax.random.fold_in(own, 3), number_of)
    giver, receiver = mixed[0:number_of // 2 * 2:2], mixed[1:number_of // 2 * 2:2]
    margin = jnp.minimum(tallies[giver] - 1, limit - tallies[receiver]) // 2
    margin = jnp.where((giver == order[0]) | (receiver == order[0]) | (tallies[receiver] == 0), 0, jnp.maximum(margin, 0))
    passed = jax.random.randint(jax.random.fold_in(own, 4), (number_of // 2,), 0, 1 << 20) % (margin + 1)
    tallies = tallies.at[giver].add(-passed).at[receiver].add(passed)
    members = jnp.searchsorted(jnp.cumsum(tallies), jnp.arange(rows * top), side="right").astype(jnp.int32)
    listing = members.reshape(top, rows).T
    listing = listing[jax.random.permutation(jax.random.fold_in(own, 1), rows)]
    rotation = jax.random.randint(jax.random.fold_in(own, 2), (rows, 1), 0, top)
    return jnp.take_along_axis(listing, (jnp.arange(top)[None, :] + rotation) % top, axis=1)


def load_shares(number_of, total, reach, slope, full):
    weights = [(1 << 20) // math.isqrt(rank ** slope) + 1 for rank in range(1, number_of + 1)]
    largest = reach if full else min(reach, max(-(-total // number_of), total * weights[0] // sum(weights)))
    least = 1 if total - largest >= number_of - 1 else 0
    counts, spare = [largest] + [least] * (number_of - 1), total - largest - least * (number_of - 1)
    while spare > 0:
        movable = [i for i in range(1, number_of) if counts[i] < largest] or [i for i in range(1, number_of) if counts[i] < reach]
        whole, left = sum([weights[i] for i in movable]), spare
        for i in movable:
            extra = min(reach - counts[i], max(1, left * weights[i] // whole), spare)
            counts[i] = counts[i] + extra
            spare = spare - extra
    return np.array(counts)


def bell_draw(rng, shape, width, most, cuts=(), held_as=jnp.bfloat16):
    drawn = width * jax.random.normal(rng, shape, jnp.float32)
    if cuts:
        drawn = drawn * shard_levels(rng, shape, cuts, -0.22, 0.18)
    return jnp.clip(drawn, -most, most).astype(held_as)


def setup_inputs(seed: int = 0, part: int = 0) -> dict:
    keys = jax.random.split(jax.random.key(seed), 12)
    own_keys = jax.random.split(jax.random.fold_in(keys[11], part), 12)
    density = bell_draw(own_keys[0], (NTILE, PT), 1.0, 6.0, ((0, 16),))
    three_center = bell_draw(own_keys[1], (NAUXB, LJ, PT, AB), (PT * LJ // 4) ** -0.5, 0.125, ((0, 16),))
    metric = draw_metric(jax.random.fold_in(jax.random.fold_in(keys[11], part), 71), part)
    fetch_owner_keys = jax.random.split(jax.random.fold_in(own_keys[3], 1), (N_TILE * REQ) // REQ)
    fetch_owner_turns = jax.random.permutation(jax.random.fold_in(own_keys[3], 3), (N_TILE * REQ) // REQ)
    fetch_owner = jax.vmap(lambda own, number: assign_block(jax.random.fold_in(own_keys[3], 2), own, number, REQ, N_TILE, 1, CAP, 2))(fetch_owner_keys, fetch_owner_turns).reshape((N_TILE * REQ, 1))
    fetch_slot = plant(jax.random.randint(own_keys[4], (N_TILE * REQ,), 0, TILE_DEV), jax.random.fold_in(own_keys[4], 1), 0, TILE_DEV - 1).astype(jnp.int32)
    basis_value = bell_draw(own_keys[5], (NBATCH, KB, TB, G), ((2 * LX * PT) ** -0.25), 1.0, ((0, 16),))
    basis_gradient = bell_draw(own_keys[6], (NBATCH, KB, 3, TB, G), (4 * (2 * LX * PT) ** -0.25), 4.0, ((0, 16),))
    pair_slot = plant(jax.random.randint(own_keys[7], (NBATCH, LX, 2), 0, KB), jax.random.fold_in(own_keys[7], 1), 0, KB - 1).astype(jnp.int32)
    base_density = jnp.clip(jnp.exp(math.log(3.0) - 2.3025851 * jax.random.uniform(own_keys[8], (NBATCH, G), jnp.float32) ** shard_levels(own_keys[8], (NBATCH, G), ((0, 16),), -0.2, 0.2)), 0.3, 3.0)
    base_kinetic = jnp.clip(jnp.exp(math.log(40.0) - 2.3025851 * jax.random.uniform(own_keys[9], (NBATCH, G), jnp.float32) ** shard_levels(own_keys[9], (NBATCH, G), ((0, 16),), -0.2, 0.2)), 4.0, 40.0)
    grid_weight = jnp.clip(jnp.exp(math.log(4.0) - 1.3862944 * jax.random.uniform(own_keys[10], (NBATCH, G), jnp.float32) ** shard_levels(own_keys[10], (NBATCH, G), ((0, 16),), -0.2, 0.2)), 1.0, 4.0)
    return {"density": density, "three_center": three_center, "metric": metric, "fetch_owner": fetch_owner, "fetch_slot": fetch_slot, "basis_value": basis_value, "basis_gradient": basis_gradient, "pair_slot": pair_slot, "base_density": base_density, "base_kinetic": base_kinetic, "grid_weight": grid_weight}


CX_COEF = 0.7385587663820224
CS_COEF = 0.026121172985233605
CTF_COEF = 2.871234000188191
KAPPA_VALUE = 0.804
MU_COEF = 0.12345679012345678
H_ZERO = 1.174

def smooth_floor(amount):
    return 0.5 * (amount + jnp.sqrt(amount * amount + 1.0))

def point_energy(dens_point, grad_square, kinetic):
    s_square = CS_COEF * grad_square / jnp.power(dens_point, 8.0 / 3.0)
    h_one = 1.0 + KAPPA_VALUE - KAPPA_VALUE / (1.0 + MU_COEF * s_square / KAPPA_VALUE)
    iso_alpha = (kinetic - grad_square / (8.0 * dens_point)) / (CTF_COEF * jnp.power(dens_point, 5.0 / 3.0))
    factor = h_one + (H_ZERO - h_one) / (1.0 + iso_alpha * iso_alpha)
    return -CX_COEF * jnp.power(dens_point, 4.0 / 3.0) * factor

def batch_potential(inputs):
    point_value, point_slope, slot_pairs, tile_rows, base_rho, base_tau, weights = inputs
    basis = jnp.concatenate([point_value[:, None], point_slope], axis=1).astype(jnp.float32)
    left_basis = basis[slot_pairs[:, 0]]
    right_basis = basis[slot_pairs[:, 1]]
    count = tile_rows.shape[0]
    tile_edge = basis.shape[2]
    start = tile_rows.astype(jnp.float32).reshape(count, tile_edge, tile_edge)

    def energy(tile_values):
        mixed_terms = jnp.einsum('rmn,rcng->rcmg', tile_values, right_basis)
        point_rho = lax.optimization_barrier(jnp.sum(left_basis[:, 0] * mixed_terms[:, 0], axis=(0, 1)))
        point_grad = lax.optimization_barrier(jnp.sum(left_basis[:, 1:] * mixed_terms[:, :1] + left_basis[:, :1] * mixed_terms[:, 1:], axis=(0, 2)))
        point_tau = 0.5 * lax.optimization_barrier(jnp.sum(left_basis[:, 1:] * mixed_terms[:, 1:], axis=(0, 1, 2)))
        dens_point = smooth_floor(base_rho + point_rho)
        kinetic = smooth_floor(base_tau + point_tau)
        grad_square = lax.optimization_barrier(jnp.sum(point_grad * point_grad, axis=0))
        return jnp.sum(weights * point_energy(dens_point, grad_square, kinetic))
    unused, pullback = jax.vjp(energy, start)
    return pullback(jnp.ones((), start.dtype))[0].reshape(count, tile_edge * tile_edge)

def reference(density, three_center, metric, fetch_owner, fetch_slot, basis_value, basis_gradient, pair_slot, base_density, base_kinetic, grid_weight):
    tile_index = (fetch_owner[:, 0] * TILE_DEV + fetch_slot).reshape(N_TILE, REQ)
    coul_rows = AUXB_DEV * LJ
    coul_index = tile_index[:, :coul_rows].reshape(NAUXB, LJ)
    xc_index = tile_index[:, coul_rows:].reshape(NBATCH, LX)

    def coulomb_block(inputs):
        block, indices, inverse = inputs
        picked = density[indices].astype(jnp.float32)
        block_float = block.astype(jnp.float32)
        source = jnp.einsum('rkp,rk->p', block_float, picked)
        fit_coef = jnp.dot(inverse, source, precision=lax.Precision.HIGHEST).astype(jnp.bfloat16)
        return jnp.einsum('rkp,p->rk', block_float, fit_coef.astype(jnp.float32))
    coul_part = lax.map(coulomb_block, (three_center, coul_index, metric))
    coulomb = jax.ops.segment_sum(coul_part.reshape(NAUXB * LJ, PT), coul_index.reshape(NAUXB * LJ), num_segments=NTILE)
    xc_tiles = density[xc_index]
    xc_part = lax.map(batch_potential, (basis_value, basis_gradient, pair_slot, xc_tiles, base_density, base_kinetic, grid_weight))
    exchange_corr = jax.ops.segment_sum(xc_part.reshape(NBATCH * LX, PT), xc_index.reshape(NBATCH * LX), num_segments=NTILE)
    return (coulomb, exchange_corr)
```

```python
import functools

import jax
import jax.numpy as jnp
from jax import lax
from jax.experimental import pallas as pl
from jax.experimental.pallas import tpu as pltpu
from jax.sharding import PartitionSpec as P

CX_COEF = 0.7385587663820224
CS_COEF = 0.026121172985233605
CTF_COEF = 2.871234000188191
KAPPA_VALUE = 0.804
MU_COEF = 0.12345679012345678
H_ZERO = 1.174

F32 = jnp.float32
BF16 = jnp.bfloat16
LANES = 128


def dot(left, right):
    return lax.dot_general(left, right, (((1,), (0,)), ((), ())), preferred_element_type=F32)


def dot_nt(left, right, precision=None):
    return lax.dot_general(
        left, right, (((1,), (1,)), ((), ())), precision=precision, preferred_element_type=F32
    )


def dot_tn(left, right):
    return lax.dot_general(left, right, (((0,), (0,)), ((), ())), preferred_element_type=F32)


def iota(shape, dim):
    return lax.broadcasted_iota(jnp.int32, shape, dim)


def one_hot(condition):
    return jnp.where(condition, 1.0, 0.0).astype(BF16)


def smooth_floor(amount):
    return 0.5 * (amount + jnp.sqrt(amount * amount + 1.0))


def point_energy(grid_rho, grad_x, grad_y, grad_z, grid_tau, base_rho, base_tau, weights):
    rho = smooth_floor(base_rho + grid_rho)
    tau = smooth_floor(base_tau + grid_tau)
    sigma = grad_x * grad_x + grad_y * grad_y + grad_z * grad_z
    root = jnp.exp(jnp.log(rho) * (1.0 / 3.0))
    five = rho * root * root
    s_square = CS_COEF * sigma / (rho * five)
    h_one = 1.0 + KAPPA_VALUE - KAPPA_VALUE / (1.0 + MU_COEF * s_square / KAPPA_VALUE)
    iso_alpha = (tau - sigma / (8.0 * rho)) / (CTF_COEF * five)
    factor = h_one + (H_ZERO - h_one) / (1.0 + iso_alpha * iso_alpha)
    return weights * (-CX_COEF * (rho * root) * factor)


def kernel(
    sizes,
    density_hbm,
    metric_hbm,
    owner_hbm,
    slot_hbm,
    pair_hbm,
    base_rho_hbm,
    base_tau_hbm,
    weight_hbm,
    three_hbm,
    value_hbm,
    slope_hbm,
    coul_out,
    xc_out,
    owner_ref,
    slot_ref,
    pair_ref,
    base_rho_ref,
    base_tau_ref,
    weight_ref,
    metric_ref,
    table,
    three,
    basis,
    left,
    spread,
    fetched,
    dense,
    dense_low,
    masks,
    takes,
    gathered,
    coul_rows_s,
    xc_rows_s,
    points,
    slopes,
    coul_send,
    xc_send,
    coul_recv,
    xc_recv,
    local_sem,
    gather_send_sem,
    gather_recv_sem,
    coul_send_sem,
    coul_recv_sem,
    xc_send_sem,
    xc_recv_sem,
):
    devices, tile_count, width, aux, listed, batches, refs, blocks, edge, grid = sizes
    coul_rows = aux * listed
    basis_rows = blocks * edge
    edge_bits = edge.bit_length() - 1
    block_bits = blocks.bit_length() - 1
    lane_bits = grid.bit_length() - 1
    total_tiles = devices * tile_count
    me = lax.axis_index("tile")

    own_rows = pl.ds(pl.multiple_of(me * tile_count, tile_count), tile_count)
    moves = [
        (density_hbm, table.at[own_rows]),
        (owner_hbm, owner_ref),
        (slot_hbm, slot_ref),
        (pair_hbm, pair_ref),
        (value_hbm, basis.at[:, :, :, 0:grid]),
    ]
    for c in range(3):
        moves.append(
            (slope_hbm.at[:, :, c], basis.at[:, :, :, (c + 1) * grid : (c + 2) * grid])
        )
    moves += [
        (three_hbm, three),
        (metric_hbm, metric_ref),
        (base_rho_hbm, base_rho_ref),
        (base_tau_hbm, base_tau_ref),
        (weight_hbm, weight_ref),
    ]
    copies = [
        pltpu.make_async_copy(source, target, local_sem.at[k])
        for k, (source, target) in enumerate(moves)
    ]

    barrier = pltpu.get_barrier_semaphore()

    def greet(shift, carry):
        peer = lax.rem(me + shift, devices)
        pl.semaphore_signal(
            barrier, inc=1, device_id={"tile": peer}, device_id_type=pl.DeviceIdType.MESH
        )
        return carry

    lax.fori_loop(1, devices, greet, 0)
    for copy in copies:
        copy.start()

    def send(source, target, send_sem, recv_sem, shift):
        return pltpu.make_async_remote_copy(
            src_ref=source,
            dst_ref=target,
            send_sem=send_sem.at[shift],
            recv_sem=recv_sem.at[shift],
            device_id={"tile": lax.rem(me + shift, devices)},
            device_id_type=pl.DeviceIdType.MESH,
        )

    def tile_rows(ref, owner):
        return ref.at[pl.ds(pl.multiple_of(owner * tile_count, tile_count), tile_count)]

    copies[0].wait()
    pl.semaphore_wait(barrier, devices - 1)

    def gather_start(shift, carry):
        send(tile_rows(table, me), tile_rows(table, me), gather_send_sem, gather_recv_sem, shift).start()
        return carry

    lax.fori_loop(1, devices, gather_start, 0)

    spread_width = edge * LANES
    row = iota((width, spread_width), 0)
    lane = iota((width, spread_width), 1)
    spread[...] = one_hot(
        (jnp.right_shift(row, edge_bits) == jnp.right_shift(lane, 7))
        & ((row & (edge - 1)) == (lane & (edge - 1)))
    )
    row = iota((basis_rows, basis_rows), 0)
    lane = iota((basis_rows, basis_rows), 1)
    order = one_hot(lane == ((row & (blocks - 1)) << edge_bits) + jnp.right_shift(row, block_bits))
    for copy in copies[1:4]:
        copy.wait()
    drop = one_hot(
        owner_ref[...] * tile_count + slot_ref[...]
        == iota((total_tiles, coul_rows + batches * refs), 0)
    )
    same = one_hot(
        iota((blocks, basis_rows), 0) == jnp.right_shift(iota((blocks, basis_rows), 1), edge_bits)
    )
    unit = one_hot(iota((blocks, blocks), 0) == iota((blocks, blocks), 1))
    for b in range(batches):
        block_row = iota((blocks, refs), 0)
        masks[b] = dot_tn(one_hot(pair_ref[b, 1:2, :] == block_row), same).astype(BF16)
        takes[b] = dot_tn(one_hot(pair_ref[b, 0:1, :] == block_row), unit).astype(BF16)
    for copy in copies[4:8]:
        copy.wait()

    def reorder(b, carry):
        left[b] = dot(order, basis[b].reshape(basis_rows, 4 * grid)).astype(BF16)
        return carry

    lax.fori_loop(0, batches, reorder, 0)

    def gather_wait(shift, carry):
        owner = lax.rem(me - shift + devices, devices)
        copy = send(tile_rows(table, me), tile_rows(table, owner), gather_send_sem, gather_recv_sem, shift)
        copy.wait_recv()
        copy.wait_send()
        return carry

    lax.fori_loop(1, devices, gather_wait, 0)

    picked = dot_tn(drop, table[...])
    coul_tiles = picked[:coul_rows]
    fetched[...] = dot(picked[coul_rows:].astype(BF16), spread[...]).astype(BF16)

    copies[8].wait()
    copies[9].wait()
    for a in range(aux):
        source = jnp.zeros((1, grid), F32)
        for r in range(listed):
            k = a * listed + r
            source = source + dot(coul_tiles[k : k + 1].astype(BF16), three[a, r])
        coef = dot_nt(source, metric_ref[a], lax.Precision.HIGHEST).astype(BF16)
        for r in range(listed):
            k = a * listed + r
            coul_rows_s[k : k + 1, :] = dot_nt(coef, three[a, r])
    part = coul_rows_s[...]
    high = part.astype(BF16)
    low = (part - high.astype(F32)).astype(BF16)
    drop_coul = drop[:, :coul_rows]
    coul_send[...] = (dot(drop_coul, high) + dot(drop_coul, low)).astype(BF16)

    def push(source, recv, send_sem, recv_sem):
        def start(shift, carry):
            peer = lax.rem(me + shift, devices)
            send(tile_rows(source, peer), recv.at[shift], send_sem, recv_sem, shift).start()
            return carry

        lax.fori_loop(1, devices, start, 0)

    def total(source, recv, send_sem, recv_sem):
        own = source[pl.ds(pl.multiple_of(me * tile_count, tile_count), tile_count), :]

        def add(shift, so_far):
            peer = lax.rem(me + shift, devices)
            copy = send(tile_rows(source, peer), recv.at[shift], send_sem, recv_sem, shift)
            copy.wait_recv()
            copy.wait_send()
            return so_far + recv[shift].astype(F32)

        return lax.fori_loop(1, devices, add, own.astype(F32))

    push(coul_send, coul_recv, coul_send_sem, coul_recv_sem)

    chunk = min(basis_rows, 128)

    def batch_rows(b):
        return pl.ds(pl.multiple_of(b * refs, refs), refs)

    copies_across = basis_rows // LANES

    def forward(b, carry):
        mask, rows = masks[b], batch_rows(b)
        place = one_hot(pair_ref[b, 0:1, :] == iota((blocks, refs), 0))
        for m in range(edge):
            part = fetched[rows, m * LANES : (m + 1) * LANES]
            wide = jnp.concatenate([part] * copies_across, axis=1) * mask
            full = dot(place, wide)
            high = full.astype(BF16)
            dense[m * blocks : (m + 1) * blocks, :] = high
            dense_low[m * blocks : (m + 1) * blocks, :] = (full - high.astype(F32)).astype(BF16)
        right = basis[b].reshape(basis_rows, 4 * grid)
        sums = [jnp.zeros((8, grid), F32) for unused in range(5)]
        for start in range(0, basis_rows, chunk):
            mixed = dot(dense[start : start + chunk, :], right)
            mixed = mixed + dot(dense_low[start : start + chunk, :], right)
            lefts = left[b, start : start + chunk, :].astype(F32)

            def part(array, c):
                return array[:, c * grid : (c + 1) * grid]

            l0, m0 = part(lefts, 0), part(mixed, 0)
            terms = [l0 * m0]
            tau = None
            for c in range(1, 4):
                lc, mc = part(lefts, c), part(mixed, c)
                terms.append(lc * m0 + l0 * mc)
                tau = lc * mc if tau is None else tau + lc * mc
            terms.append(tau)
            for q in range(5):
                sums[q] = sums[q] + jnp.sum(terms[q].reshape(chunk // 8, 8, grid), axis=0)
        for q in range(5):
            points[q, pl.ds(b, 1), :] = jnp.sum(sums[q], axis=0, keepdims=True)
        return carry

    lax.fori_loop(0, batches, forward, 0)

    for copy in copies[10:]:
        copy.wait()
    base_rho, base_tau, weights = base_rho_ref[...], base_tau_ref[...], weight_ref[...]

    def energy(grid_rho, grad_x, grad_y, grad_z, grid_tau):
        return point_energy(
            grid_rho, grad_x, grad_y, grad_z, grid_tau, base_rho, base_tau, weights
        )

    values = [points[q] for q in range(5)]
    values[4] = 0.5 * values[4]
    unused, pullback = jax.vjp(energy, *values)
    found = pullback(jnp.ones_like(weights))
    for q in range(5):
        slopes[q] = 0.5 * found[q] if q == 4 else found[q]

    def backward(b, carry):
        mask, take, rows = masks[b].astype(F32), takes[b], batch_rows(b)
        by = [slopes[q, pl.ds(b, 1), :] for q in range(5)]
        right = basis[b].reshape(basis_rows, 4 * grid).astype(F32)
        part = [right[:, c * grid : (c + 1) * grid] for c in range(4)]
        bent = [by[0] * part[0] + by[1] * part[1] + by[2] * part[2] + by[3] * part[3]]
        for c in range(1, 4):
            bent.append(by[c] * part[0] + by[4] * part[c])
        bent = jnp.concatenate([each.astype(BF16) for each in bent], axis=1)
        per = max(1, chunk // blocks)
        for m in range(0, edge, per):
            outer = dot_nt(left[b, m * blocks : (m + per) * blocks, :], bent).astype(BF16)
            for s in range(per):
                own = dot(take, outer[s * blocks : (s + 1) * blocks]) * mask
                folded = own[:, :LANES]
                for q in range(1, copies_across):
                    folded = folded + own[:, q * LANES : (q + 1) * LANES]
                gathered[:, (m + s) * LANES : (m + s + 1) * LANES] = folded.astype(BF16)
        xc_rows_s[rows, :] = dot_nt(gathered[...], spread[...]).astype(BF16)
        return carry

    lax.fori_loop(0, batches, backward, 0)
    xc_send[...] = dot(drop[:, coul_rows:], xc_rows_s[...]).astype(BF16)
    push(xc_send, xc_recv, xc_send_sem, xc_recv_sem)
    coul_out[...] = total(coul_send, coul_recv, coul_send_sem, coul_recv_sem)
    xc_out[...] = total(xc_send, xc_recv, xc_send_sem, xc_recv_sem)


def body(
    density,
    three_center,
    metric,
    fetch_owner,
    fetch_slot,
    basis_value,
    basis_gradient,
    pair_slot,
    base_density,
    base_kinetic,
    grid_weight,
):
    devices = lax.axis_size("tile")
    tile_count, width = density.shape
    aux, listed = three_center.shape[:2]
    batches, refs = pair_slot.shape[:2]
    blocks, edge, grid = basis_value.shape[1:]
    coul_rows = aux * listed
    total_refs = coul_rows + batches * refs
    sizes = (devices, tile_count, width, aux, listed, batches, refs, blocks, edge, grid)
    vmem = pl.BlockSpec(memory_space=pltpu.VMEM)
    far = pl.BlockSpec(memory_space=pl.ANY)
    total_tiles = devices * tile_count
    basis_rows = blocks * edge
    out = jax.ShapeDtypeStruct((tile_count, width), F32)
    semaphores = pltpu.SemaphoreType.DMA((devices,))
    return pl.pallas_call(
        functools.partial(kernel, sizes),
        out_shape=(out, out),
        in_specs=[far] * 11,
        out_specs=(vmem, vmem),
        scratch_shapes=[
            pltpu.VMEM((1, total_refs), jnp.int32),
            pltpu.VMEM((1, total_refs), jnp.int32),
            pltpu.VMEM((batches, 2, refs), jnp.int32),
            pltpu.VMEM((batches, grid), F32),
            pltpu.VMEM((batches, grid), F32),
            pltpu.VMEM((batches, grid), F32),
            pltpu.VMEM(metric.shape, F32),
            pltpu.VMEM((total_tiles, width), BF16),
            pltpu.VMEM(three_center.shape, BF16),
            pltpu.VMEM((batches, blocks, edge, 4 * grid), BF16),
            pltpu.VMEM((batches, basis_rows, 4 * grid), BF16),
            pltpu.VMEM((width, edge * LANES), BF16),
            pltpu.VMEM((batches * refs, edge * LANES), BF16),
            pltpu.VMEM((basis_rows, basis_rows), BF16),
            pltpu.VMEM((basis_rows, basis_rows), BF16),
            pltpu.VMEM((batches, refs, basis_rows), BF16),
            pltpu.VMEM((batches, refs, blocks), BF16),
            pltpu.VMEM((refs, edge * LANES), BF16),
            pltpu.VMEM((coul_rows, width), F32),
            pltpu.VMEM((batches * refs, width), BF16),
            pltpu.VMEM((5, batches, grid), F32),
            pltpu.VMEM((5, batches, grid), F32),
            pltpu.VMEM((total_tiles, width), BF16),
            pltpu.VMEM((total_tiles, width), BF16),
            pltpu.VMEM((devices, tile_count, width), BF16),
            pltpu.VMEM((devices, tile_count, width), BF16),
            pltpu.SemaphoreType.DMA((13,)),
            semaphores,
            semaphores,
            semaphores,
            semaphores,
            semaphores,
            semaphores,
        ],
        compiler_params=pltpu.CompilerParams(
            collective_id=0, has_side_effects=True, vmem_limit_bytes=60 * 1024 * 1024
        ),
        name="fock_build",
    )(
        density,
        metric,
        fetch_owner.reshape(1, total_refs),
        fetch_slot.reshape(1, total_refs),
        jnp.swapaxes(pair_slot, 1, 2),
        base_density,
        base_kinetic,
        grid_weight,
        three_center,
        basis_value,
        basis_gradient,
    )


def solution(mesh):
    in_specs = (
        P(("parts", "tile"), None),
        P(("parts", "tile"), None, None, None),
        P(("parts", "tile"), None, None),
        P(("parts", "tile"), None),
        P(("parts", "tile")),
        P(("parts", "tile"), None, None, None),
        P(("parts", "tile"), None, None, None, None),
        P(("parts", "tile"), None, None),
        P(("parts", "tile"), None),
        P(("parts", "tile"), None),
        P(("parts", "tile"), None),
    )
    out_specs = (P(("parts", "tile"), None), P(("parts", "tile"), None))
    return jax.shard_map(body, mesh=mesh, in_specs=in_specs, out_specs=out_specs, check_vma=False)
```

```python
import functools

import jax
import jax.numpy as jnp
from jax import lax
from jax.experimental import pallas as pl
from jax.experimental.pallas import tpu as pltpu
from jax.sharding import PartitionSpec as P

CX_COEF = 0.7385587663820224
CS_COEF = 0.026121172985233605
CTF_COEF = 2.871234000188191
KAPPA_VALUE = 0.804
MU_COEF = 0.12345679012345678
H_ZERO = 1.174

F32 = jnp.float32
BF16 = jnp.bfloat16
LANES = 128


def dot(left, right):
    return lax.dot_general(left, right, (((1,), (0,)), ((), ())), preferred_element_type=F32)


def dot_nt(left, right, precision=None):
    return lax.dot_general(
        left, right, (((1,), (1,)), ((), ())), precision=precision, preferred_element_type=F32
    )


def dot_tn(left, right):
    return lax.dot_general(left, right, (((0,), (0,)), ((), ())), preferred_element_type=F32)


def iota(shape, dim):
    return lax.broadcasted_iota(jnp.int32, shape, dim)


def one_hot(condition):
    return jnp.where(condition, 1.0, 0.0).astype(BF16)


def smooth_floor(amount):
    return 0.5 * (amount + jnp.sqrt(amount * amount + 1.0))


def point_energy(grid_rho, grad_x, grad_y, grad_z, grid_tau, base_rho, base_tau, weights):
    rho = smooth_floor(base_rho + grid_rho)
    tau = smooth_floor(base_tau + grid_tau)
    sigma = grad_x * grad_x + grad_y * grad_y + grad_z * grad_z
    root = jnp.exp(jnp.log(rho) * (1.0 / 3.0))
    five = rho * root * root
    s_square = CS_COEF * sigma / (rho * five)
    h_one = 1.0 + KAPPA_VALUE - KAPPA_VALUE / (1.0 + MU_COEF * s_square / KAPPA_VALUE)
    iso_alpha = (tau - sigma / (8.0 * rho)) / (CTF_COEF * five)
    factor = h_one + (H_ZERO - h_one) / (1.0 + iso_alpha * iso_alpha)
    return weights * (-CX_COEF * (rho * root) * factor)


def kernel(
    sizes,
    density_hbm,
    metric_hbm,
    owner_hbm,
    slot_hbm,
    pair_hbm,
    base_rho_hbm,
    base_tau_hbm,
    weight_hbm,
    three_hbm,
    value_hbm,
    slope_hbm,
    both_out,
    owner_ref,
    slot_ref,
    pair_ref,
    base_rho_ref,
    base_tau_ref,
    weight_ref,
    metric_ref,
    table,
    three,
    basis,
    left,
    spread,
    gather_up,
    pick,
    mixed_s,
    outer_s,
    fetched,
    dense,
    dense_low,
    masks,
    takes,
    gathered,
    coul_rows_s,
    points,
    slopes,
    coul_send,
    xc_send,
    coul_recv,
    xc_recv,
    local_sem,
    gather_send_sem,
    gather_recv_sem,
    coul_send_sem,
    coul_recv_sem,
    xc_send_sem,
    xc_recv_sem,
):
    devices, tile_count, width, aux, listed, batches, refs, blocks, edge, grid = sizes
    coul_rows = aux * listed
    total_refs = coul_rows + batches * refs
    basis_rows = blocks * edge
    edge_bits = edge.bit_length() - 1
    block_bits = blocks.bit_length() - 1
    lane_bits = grid.bit_length() - 1
    total_tiles = devices * tile_count
    me = lax.axis_index("tile")

    own_rows = pl.ds(pl.multiple_of(me * tile_count, tile_count), tile_count)
    moves = [
        (density_hbm, table.at[own_rows]),
        (owner_hbm, owner_ref),
        (slot_hbm, slot_ref),
        (pair_hbm, pair_ref),
        (value_hbm, basis.at[:, :, :, 0:grid]),
    ]
    for c in range(3):
        moves.append(
            (slope_hbm.at[:, :, c], basis.at[:, :, :, (c + 1) * grid : (c + 2) * grid])
        )
    moves += [
        (three_hbm, three),
        (metric_hbm, metric_ref),
        (base_rho_hbm, base_rho_ref),
        (base_tau_hbm, base_tau_ref),
        (weight_hbm, weight_ref),
    ]
    copies = [
        pltpu.make_async_copy(source, target, local_sem.at[k])
        for k, (source, target) in enumerate(moves)
    ]

    barrier = pltpu.get_barrier_semaphore()

    def greet(shift, carry):
        peer = lax.rem(me + shift, devices)
        pl.semaphore_signal(
            barrier, inc=1, device_id={"tile": peer}, device_id_type=pl.DeviceIdType.MESH
        )
        return carry

    lax.fori_loop(1, devices, greet, 0)
    for copy in copies:
        copy.start()

    def send(source, target, send_sem, recv_sem, shift):
        return pltpu.make_async_remote_copy(
            src_ref=source,
            dst_ref=target,
            send_sem=send_sem.at[shift],
            recv_sem=recv_sem.at[shift],
            device_id={"tile": lax.rem(me + shift, devices)},
            device_id_type=pl.DeviceIdType.MESH,
        )

    def tile_rows(ref, owner):
        return ref.at[pl.ds(pl.multiple_of(owner * tile_count, tile_count), tile_count)]

    spread[...] = jnp.zeros_like(spread)
    repeat = one_hot(iota((edge, LANES), 0) == (iota((edge, LANES), 1) & (edge - 1)))
    step = jnp.where(
        (iota((LANES, width), 0) & (edge - 1)) == (iota((LANES, width), 1) & (edge - 1)), 1.0, 0.0
    )
    which = jnp.right_shift(iota((1, width), 1), edge_bits)
    for m in range(edge):
        spread[m * edge : (m + 1) * edge, m * LANES : (m + 1) * LANES] = repeat
        gather_up[m * LANES : (m + 1) * LANES, :] = (
            step * jnp.where(which == m, 1.0, 0.0)
        ).astype(BF16)
    lane = iota((1, basis_rows), 1)
    order = one_hot(
        iota((basis_rows, basis_rows), 0)
        == ((lane & (edge - 1)) << block_bits) + jnp.right_shift(lane, edge_bits)
    )
    for copy in copies[1:4]:
        copy.wait()
    drop = one_hot(
        owner_ref[...] * tile_count + slot_ref[...].reshape(1, total_refs)
        == iota((total_tiles, coul_rows + batches * refs), 0)
    )
    same = one_hot(
        iota((blocks, basis_rows), 0) == jnp.right_shift(iota((blocks, basis_rows), 1), edge_bits)
    )
    unit = one_hot(iota((blocks, blocks), 0) == iota((blocks, blocks), 1))
    for b in range(batches):
        block_row = iota((blocks, refs), 0)
        masks[b] = dot_tn(one_hot(pair_ref[b, 1:2, :] == block_row), same).astype(BF16)
        takes[b] = dot_tn(one_hot(pair_ref[b, 0:1, :] == block_row), unit).astype(BF16)
    pick[...] = jnp.transpose(drop.astype(F32)).astype(BF16)
    copies[0].wait()
    pl.semaphore_wait(barrier, devices - 1)

    def gather_start(shift, carry):
        send(tile_rows(table, me), tile_rows(table, me), gather_send_sem, gather_recv_sem, shift).start()
        return carry

    lax.fori_loop(1, devices, gather_start, 0)

    for copy in copies[4:8]:
        copy.wait()

    def reorder(b, carry):
        left[b] = dot(order, basis[b].reshape(basis_rows, 4 * grid)).astype(BF16)
        return carry

    lax.fori_loop(0, batches, reorder, 0, unroll=True)

    def gather_wait(shift, carry):
        owner = lax.rem(me - shift + devices, devices)
        copy = send(tile_rows(table, me), tile_rows(table, owner), gather_send_sem, gather_recv_sem, shift)
        copy.wait_recv()
        copy.wait_send()
        return carry

    lax.fori_loop(1, devices, gather_wait, 0)

    picked = dot(pick[...], table[...])
    coul_tiles = picked[:coul_rows]
    fetched[...] = dot(picked[coul_rows:].astype(BF16), spread[...]).astype(BF16)

    copies[8].wait()
    copies[9].wait()
    for a in range(aux):
        source = jnp.zeros((2, 2 * grid), F32)
        for r in range(0, listed, 2):
            k = a * listed + r
            pair = jnp.concatenate([three[a, r], three[a, r + 1]], axis=1)
            source = source + dot(coul_tiles[k : k + 2].astype(BF16), pair)
        source = source[0:1, :grid] + source[1:2, grid:]
        coef = dot_nt(source, metric_ref[a], lax.Precision.HIGHEST)
        none = jnp.zeros_like(coef)
        coef = jnp.concatenate(
            [jnp.concatenate([coef, none], axis=1), jnp.concatenate([none, coef], axis=1)], axis=0
        ).astype(BF16)
        for r in range(0, listed, 2):
            k = a * listed + r
            pair = jnp.concatenate([three[a, r], three[a, r + 1]], axis=1)
            coul_rows_s[k : k + 2, :] = dot_nt(coef, pair)
    part = coul_rows_s[...]
    high = part.astype(BF16)
    low = (part - high.astype(F32)).astype(BF16)
    drop_coul = drop[:, :coul_rows]
    coul_send[...] = (dot(drop_coul, high) + dot(drop_coul, low)).astype(BF16)

    def push(source, recv, send_sem, recv_sem):
        def start(shift, carry):
            peer = lax.rem(me + shift, devices)
            send(tile_rows(source, peer), recv.at[shift], send_sem, recv_sem, shift).start()
            return carry

        lax.fori_loop(1, devices, start, 0)

    def total(source, recv, send_sem, recv_sem):
        own = source[pl.ds(pl.multiple_of(me * tile_count, tile_count), tile_count), :]

        def add(shift, so_far):
            peer = lax.rem(me + shift, devices)
            copy = send(tile_rows(source, peer), recv.at[shift], send_sem, recv_sem, shift)
            copy.wait_recv()
            copy.wait_send()
            return so_far + recv[shift].astype(F32)

        return lax.fori_loop(1, devices, add, own.astype(F32))

    push(coul_send, coul_recv, coul_send_sem, coul_recv_sem)

    chunk = min(basis_rows, 128)

    def batch_rows(b):
        return pl.ds(pl.multiple_of(b * refs, refs), refs)

    copies_across = basis_rows // LANES

    def forward(b, carry):
        mask, rows = masks[b], batch_rows(b)
        place = one_hot(pair_ref[b, 0:1, :] == iota((blocks, refs), 0))
        for m in range(edge):
            part = fetched[rows, m * LANES : (m + 1) * LANES]
            wide = jnp.concatenate([part] * copies_across, axis=1) * mask
            full = dot(place, wide)
            high = full.astype(BF16)
            dense[m * blocks : (m + 1) * blocks, :] = high
            dense_low[m * blocks : (m + 1) * blocks, :] = (full - high.astype(F32)).astype(BF16)
        right = basis[b].reshape(basis_rows, 4 * grid)
        mixed_s[...] = dot(dense[...], right) + dot(dense_low[...], right)
        sums = [jnp.zeros((8, grid), F32) for unused in range(5)]
        for start in range(0, basis_rows, chunk):
            mixed = mixed_s[start : start + chunk, :]
            lefts = left[b, start : start + chunk, :].astype(F32)

            def part(array, c):
                return array[:, c * grid : (c + 1) * grid]

            l0, m0 = part(lefts, 0), part(mixed, 0)
            terms = [l0 * m0]
            tau = None
            for c in range(1, 4):
                lc, mc = part(lefts, c), part(mixed, c)
                terms.append(lc * m0 + l0 * mc)
                tau = lc * mc if tau is None else tau + lc * mc
            terms.append(tau)
            for q in range(5):
                sums[q] = sums[q] + jnp.sum(terms[q].reshape(chunk // 8, 8, grid), axis=0)
        for q in range(5):
            points[q, pl.ds(b, 1), :] = jnp.sum(sums[q], axis=0, keepdims=True)
        return carry

    lax.fori_loop(0, batches, forward, 0, unroll=True)

    for copy in copies[10:]:
        copy.wait()
    base_rho, base_tau, weights = base_rho_ref[...], base_tau_ref[...], weight_ref[...]

    def energy(grid_rho, grad_x, grad_y, grad_z, grid_tau):
        return point_energy(
            grid_rho, grad_x, grad_y, grad_z, grid_tau, base_rho, base_tau, weights
        )

    values = [points[q] for q in range(5)]
    values[4] = 0.5 * values[4]
    unused, pullback = jax.vjp(energy, *values)
    found = pullback(jnp.ones_like(weights))
    for q in range(5):
        slopes[q] = 0.5 * found[q] if q == 4 else found[q]

    def backward(b, carry):
        mask, take, rows = masks[b].astype(F32), takes[b], batch_rows(b)
        by = [slopes[q, pl.ds(b, 1), :] for q in range(5)]
        right = basis[b].reshape(basis_rows, 4 * grid).astype(F32)
        part = [right[:, c * grid : (c + 1) * grid] for c in range(4)]
        bent = [by[0] * part[0] + by[1] * part[1] + by[2] * part[2] + by[3] * part[3]]
        for c in range(1, 4):
            bent.append(by[c] * part[0] + by[4] * part[c])
        bent = jnp.concatenate([each.astype(BF16) for each in bent], axis=1)
        outer_s[...] = dot_nt(left[b], bent).astype(BF16)
        for m in range(edge):
            own = dot(take, outer_s[m * blocks : (m + 1) * blocks, :]) * mask
            folded = own[:, :LANES]
            for q in range(1, copies_across):
                folded = folded + own[:, q * LANES : (q + 1) * LANES]
            gathered[rows, m * LANES : (m + 1) * LANES] = folded.astype(BF16)
        return carry

    lax.fori_loop(0, batches, backward, 0, unroll=True)
    xc_rows = dot(gathered[...], gather_up[...]).astype(BF16)
    xc_send[...] = dot(drop[:, coul_rows:], xc_rows).astype(BF16)
    push(xc_send, xc_recv, xc_send_sem, xc_recv_sem)
    both_out[0] = total(coul_send, coul_recv, coul_send_sem, coul_recv_sem)
    both_out[1] = total(xc_send, xc_recv, xc_send_sem, xc_recv_sem)


def part_outputs(both_ref, coul_ref, xc_ref, sem):
    copies = [
        pltpu.make_async_copy(both_ref.at[0], coul_ref, sem.at[0]),
        pltpu.make_async_copy(both_ref.at[1], xc_ref, sem.at[1]),
    ]
    for copy in copies:
        copy.start()
    for copy in copies:
        copy.wait()


def body(
    density,
    three_center,
    metric,
    fetch_owner,
    fetch_slot,
    basis_value,
    basis_gradient,
    pair_slot,
    base_density,
    base_kinetic,
    grid_weight,
):
    devices = lax.axis_size("tile")
    tile_count, width = density.shape
    aux, listed = three_center.shape[:2]
    batches, refs = pair_slot.shape[:2]
    blocks, edge, grid = basis_value.shape[1:]
    coul_rows = aux * listed
    total_refs = coul_rows + batches * refs
    sizes = (devices, tile_count, width, aux, listed, batches, refs, blocks, edge, grid)
    vmem = pl.BlockSpec(memory_space=pltpu.VMEM)
    far = pl.BlockSpec(memory_space=pl.ANY)
    total_tiles = devices * tile_count
    basis_rows = blocks * edge
    out = jax.ShapeDtypeStruct((tile_count, width), F32)
    semaphores = pltpu.SemaphoreType.DMA((devices,))
    both = pl.pallas_call(
        functools.partial(kernel, sizes),
        out_shape=jax.ShapeDtypeStruct((2, tile_count, width), F32),
        in_specs=[far] * 11,
        out_specs=vmem,
        scratch_shapes=[
            pltpu.VMEM((1, total_refs), jnp.int32),
            pltpu.VMEM((total_refs,), jnp.int32),
            pltpu.VMEM((batches, 2, refs), jnp.int32),
            pltpu.VMEM((batches, grid), F32),
            pltpu.VMEM((batches, grid), F32),
            pltpu.VMEM((batches, grid), F32),
            pltpu.VMEM(metric.shape, F32),
            pltpu.VMEM((total_tiles, width), BF16),
            pltpu.VMEM(three_center.shape, BF16),
            pltpu.VMEM((batches, blocks, edge, 4 * grid), BF16),
            pltpu.VMEM((batches, basis_rows, 4 * grid), BF16),
            pltpu.VMEM((width, edge * LANES), BF16),
            pltpu.VMEM((edge * LANES, width), BF16),
            pltpu.VMEM((total_refs, total_tiles), BF16),
            pltpu.VMEM((basis_rows, 4 * grid), F32),
            pltpu.VMEM((basis_rows, basis_rows), BF16),
            pltpu.VMEM((batches * refs, edge * LANES), BF16),
            pltpu.VMEM((basis_rows, basis_rows), BF16),
            pltpu.VMEM((basis_rows, basis_rows), BF16),
            pltpu.VMEM((batches, refs, basis_rows), BF16),
            pltpu.VMEM((batches, refs, blocks), BF16),
            pltpu.VMEM((batches * refs, edge * LANES), BF16),
            pltpu.VMEM((coul_rows, width), F32),
            pltpu.VMEM((5, batches, grid), F32),
            pltpu.VMEM((5, batches, grid), F32),
            pltpu.VMEM((total_tiles, width), BF16),
            pltpu.VMEM((total_tiles, width), BF16),
            pltpu.VMEM((devices, tile_count, width), BF16),
            pltpu.VMEM((devices, tile_count, width), BF16),
            pltpu.SemaphoreType.DMA((13,)),
            semaphores,
            semaphores,
            semaphores,
            semaphores,
            semaphores,
            semaphores,
        ],
        compiler_params=pltpu.CompilerParams(
            collective_id=0, has_side_effects=True, vmem_limit_bytes=60 * 1024 * 1024
        ),
        name="fock_build",
    )(
        density,
        metric,
        fetch_owner.reshape(1, total_refs),
        fetch_slot,
        jnp.swapaxes(pair_slot, 1, 2),
        base_density,
        base_kinetic,
        grid_weight,
        three_center,
        basis_value,
        basis_gradient,
    )
    return pl.pallas_call(
        part_outputs,
        out_shape=(out, out),
        in_specs=[far],
        out_specs=(far, far),
        scratch_shapes=[pltpu.SemaphoreType.DMA((2,))],
        name="outputs",
    )(both)


def solution(mesh):
    in_specs = (
        P(("parts", "tile"), None),
        P(("parts", "tile"), None, None, None),
        P(("parts", "tile"), None, None),
        P(("parts", "tile"), None),
        P(("parts", "tile")),
        P(("parts", "tile"), None, None, None),
        P(("parts", "tile"), None, None, None, None),
        P(("parts", "tile"), None, None),
        P(("parts", "tile"), None),
        P(("parts", "tile"), None),
        P(("parts", "tile"), None),
    )
    out_specs = (P(("parts", "tile"), None), P(("parts", "tile"), None))
    return jax.shard_map(body, mesh=mesh, in_specs=in_specs, out_specs=out_specs, check_vma=False)
```

```python
import functools

import jax
import jax.numpy as jnp
from jax import lax
from jax.experimental import pallas as pl
from jax.experimental.pallas import tpu as pltpu
from jax.sharding import PartitionSpec as P

CX_COEF = 0.7385587663820224
CS_COEF = 0.026121172985233605
CTF_COEF = 2.871234000188191
KAPPA_VALUE = 0.804
MU_COEF = 0.12345679012345678
H_ZERO = 1.174

F32 = jnp.float32
BF16 = jnp.bfloat16
LANES = 128


def dot(left, right):
    return lax.dot_general(left, right, (((1,), (0,)), ((), ())), preferred_element_type=F32)


def dot_nt(left, right, precision=None):
    return lax.dot_general(
        left, right, (((1,), (1,)), ((), ())), precision=precision, preferred_element_type=F32
    )


def dot_tn(left, right):
    return lax.dot_general(left, right, (((0,), (0,)), ((), ())), preferred_element_type=F32)


def iota(shape, dim):
    return lax.broadcasted_iota(jnp.int32, shape, dim)


def one_hot(condition):
    return jnp.where(condition, 1.0, 0.0).astype(BF16)


def smooth_floor(amount):
    return 0.5 * (amount + jnp.sqrt(amount * amount + 1.0))


def point_energy(grid_rho, grad_x, grad_y, grad_z, grid_tau, base_rho, base_tau, weights):
    rho = smooth_floor(base_rho + grid_rho)
    tau = smooth_floor(base_tau + grid_tau)
    sigma = grad_x * grad_x + grad_y * grad_y + grad_z * grad_z
    root = jnp.exp(jnp.log(rho) * (1.0 / 3.0))
    five = rho * root * root
    s_square = CS_COEF * sigma / (rho * five)
    h_one = 1.0 + KAPPA_VALUE - KAPPA_VALUE / (1.0 + MU_COEF * s_square / KAPPA_VALUE)
    iso_alpha = (tau - sigma / (8.0 * rho)) / (CTF_COEF * five)
    factor = h_one + (H_ZERO - h_one) / (1.0 + iso_alpha * iso_alpha)
    return weights * (-CX_COEF * (rho * root) * factor)


def kernel(
    sizes,
    density_hbm,
    metric_hbm,
    owner_hbm,
    slot_hbm,
    pair_hbm,
    base_rho_hbm,
    base_tau_hbm,
    weight_hbm,
    three_hbm,
    value_hbm,
    slope_hbm,
    both_out,
    owner_ref,
    slot_ref,
    pair_ref,
    base_rho_ref,
    base_tau_ref,
    weight_ref,
    metric_ref,
    table,
    three,
    basis,
    left,
    spread,
    gather_up,
    pick,
    mixed_s,
    outer_s,
    fetched,
    dense,
    dense_low,
    masks,
    takes,
    gathered,
    coul_rows_s,
    points,
    slopes,
    coul_send,
    xc_send,
    coul_recv,
    xc_recv,
    local_sem,
    gather_send_sem,
    gather_recv_sem,
    coul_send_sem,
    coul_recv_sem,
    xc_send_sem,
    xc_recv_sem,
):
    devices, tile_count, width, aux, listed, batches, refs, blocks, edge, grid = sizes
    coul_rows = aux * listed
    total_refs = coul_rows + batches * refs
    basis_rows = blocks * edge
    edge_bits = edge.bit_length() - 1
    block_bits = blocks.bit_length() - 1
    lane_bits = grid.bit_length() - 1
    total_tiles = devices * tile_count
    me = lax.axis_index("tile")

    own_rows = pl.ds(pl.multiple_of(me * tile_count, tile_count), tile_count)
    moves = [
        (density_hbm, table.at[own_rows]),
        (owner_hbm, owner_ref),
        (slot_hbm, slot_ref),
        (pair_hbm, pair_ref),
        (value_hbm, basis.at[:, :, :, 0:grid]),
    ]
    for c in range(3):
        moves.append(
            (slope_hbm.at[:, :, c], basis.at[:, :, :, (c + 1) * grid : (c + 2) * grid])
        )
    moves += [
        (three_hbm, three),
        (metric_hbm, metric_ref),
        (base_rho_hbm, base_rho_ref),
        (base_tau_hbm, base_tau_ref),
        (weight_hbm, weight_ref),
    ]
    copies = [
        pltpu.make_async_copy(source, target, local_sem.at[k])
        for k, (source, target) in enumerate(moves)
    ]

    barrier = pltpu.get_barrier_semaphore()

    def greet(shift, carry):
        peer = lax.rem(me + shift, devices)
        pl.semaphore_signal(
            barrier, inc=1, device_id={"tile": peer}, device_id_type=pl.DeviceIdType.MESH
        )
        return carry

    lax.fori_loop(1, devices, greet, 0)
    for copy in copies:
        copy.start()

    def send(source, target, send_sem, recv_sem, shift):
        return pltpu.make_async_remote_copy(
            src_ref=source,
            dst_ref=target,
            send_sem=send_sem.at[shift],
            recv_sem=recv_sem.at[shift],
            device_id={"tile": lax.rem(me + shift, devices)},
            device_id_type=pl.DeviceIdType.MESH,
        )

    def tile_rows(ref, owner):
        return ref.at[pl.ds(pl.multiple_of(owner * tile_count, tile_count), tile_count)]

    spread[...] = jnp.zeros_like(spread)
    repeat = one_hot(iota((edge, LANES), 0) == (iota((edge, LANES), 1) & (edge - 1)))
    step = jnp.where(
        (iota((LANES, width), 0) & (edge - 1)) == (iota((LANES, width), 1) & (edge - 1)), 1.0, 0.0
    )
    which = jnp.right_shift(iota((1, width), 1), edge_bits)
    for m in range(edge):
        spread[m * edge : (m + 1) * edge, m * LANES : (m + 1) * LANES] = repeat
        gather_up[m * LANES : (m + 1) * LANES, :] = (
            step * jnp.where(which == m, 1.0, 0.0)
        ).astype(BF16)
    lane = iota((1, basis_rows), 1)
    order = one_hot(
        iota((basis_rows, basis_rows), 0)
        == ((lane & (edge - 1)) << block_bits) + jnp.right_shift(lane, edge_bits)
    )
    for copy in copies[1:4]:
        copy.wait()
    drop = one_hot(
        owner_ref[...] * tile_count + slot_ref[...].reshape(1, total_refs)
        == iota((total_tiles, coul_rows + batches * refs), 0)
    )
    same = one_hot(
        iota((blocks, basis_rows), 0) == jnp.right_shift(iota((blocks, basis_rows), 1), edge_bits)
    )
    unit = one_hot(iota((blocks, blocks), 0) == iota((blocks, blocks), 1))
    for b in range(batches):
        block_row = iota((blocks, refs), 0)
        masks[b] = dot_tn(one_hot(pair_ref[b, 1:2, :] == block_row), same).astype(BF16)
        takes[b] = dot_tn(one_hot(pair_ref[b, 0:1, :] == block_row), unit).astype(BF16)
    pick[...] = jnp.transpose(drop.astype(F32)).astype(BF16)
    copies[0].wait()
    pl.semaphore_wait(barrier, devices - 1)

    def gather_start(shift, carry):
        send(tile_rows(table, me), tile_rows(table, me), gather_send_sem, gather_recv_sem, shift).start()
        return carry

    lax.fori_loop(1, devices, gather_start, 0)

    for copy in copies[4:8]:
        copy.wait()

    def reorder(b, carry):
        left[b] = dot(order, basis[b].reshape(basis_rows, 4 * grid)).astype(BF16)
        return carry

    lax.fori_loop(0, batches, reorder, 0, unroll=True)

    def gather_wait(shift, carry):
        owner = lax.rem(me - shift + devices, devices)
        copy = send(tile_rows(table, me), tile_rows(table, owner), gather_send_sem, gather_recv_sem, shift)
        copy.wait_recv()
        copy.wait_send()
        return carry

    lax.fori_loop(1, devices, gather_wait, 0)

    picked = dot(pick[...], table[...])
    coul_tiles = picked[:coul_rows]
    fetched[...] = dot(picked[coul_rows:].astype(BF16), spread[...]).astype(BF16)

    copies[8].wait()
    copies[9].wait()
    def tile_pair(k):
        a, r = divmod(k, listed)
        return jnp.concatenate([three[a, r], three[a, r + 1]], axis=1)

    coul_tiles = coul_tiles.astype(BF16)
    sources = []
    for a in range(aux):
        source = jnp.zeros((2, 2 * grid), F32)
        for k in range(a * listed, (a + 1) * listed, 2):
            source = source + dot(coul_tiles[k : k + 2], tile_pair(k))
        sources.append(source[0:1, :grid] + source[1:2, grid:])
    coefs = []
    for a in range(aux):
        coef = dot_nt(sources[a], metric_ref[a], lax.Precision.HIGHEST)
        none = jnp.zeros_like(coef)
        coefs.append(
            jnp.concatenate(
                [jnp.concatenate([coef, none], axis=1), jnp.concatenate([none, coef], axis=1)],
                axis=0,
            ).astype(BF16)
        )
    for k in range(0, coul_rows, 2):
        coul_rows_s[k : k + 2, :] = dot_nt(coefs[k // listed], tile_pair(k))
    part = coul_rows_s[...]
    high = part.astype(BF16)
    low = (part - high.astype(F32)).astype(BF16)
    drop_coul = drop[:, :coul_rows]
    coul_send[...] = (dot(drop_coul, high) + dot(drop_coul, low)).astype(BF16)

    def push(source, recv, send_sem, recv_sem):
        def start(shift, carry):
            peer = lax.rem(me + shift, devices)
            send(tile_rows(source, peer), recv.at[shift], send_sem, recv_sem, shift).start()
            return carry

        lax.fori_loop(1, devices, start, 0)

    def total(source, recv, send_sem, recv_sem):
        own = source[pl.ds(pl.multiple_of(me * tile_count, tile_count), tile_count), :]

        def add(shift, so_far):
            peer = lax.rem(me + shift, devices)
            copy = send(tile_rows(source, peer), recv.at[shift], send_sem, recv_sem, shift)
            copy.wait_recv()
            copy.wait_send()
            return so_far + recv[shift].astype(F32)

        return lax.fori_loop(1, devices, add, own.astype(F32))

    push(coul_send, coul_recv, coul_send_sem, coul_recv_sem)

    chunk = min(basis_rows, 128)

    def batch_rows(b):
        return pl.ds(pl.multiple_of(b * refs, refs), refs)

    copies_across = basis_rows // LANES

    def forward(b, carry):
        mask, rows = masks[b], batch_rows(b)
        place = one_hot(pair_ref[b, 0:1, :] == iota((blocks, refs), 0))
        for m in range(edge):
            part = fetched[rows, m * LANES : (m + 1) * LANES]
            wide = jnp.concatenate([part] * copies_across, axis=1) * mask
            full = dot(place, wide)
            high = full.astype(BF16)
            dense[m * blocks : (m + 1) * blocks, :] = high
            dense_low[m * blocks : (m + 1) * blocks, :] = (full - high.astype(F32)).astype(BF16)
        right = basis[b].reshape(basis_rows, 4 * grid)
        mixed_s[...] = dot(dense[...], right) + dot(dense_low[...], right)
        sums = [jnp.zeros((8, grid), F32) for unused in range(5)]
        for start in range(0, basis_rows, chunk):
            mixed = mixed_s[start : start + chunk, :]
            lefts = left[b, start : start + chunk, :].astype(F32)

            def part(array, c):
                return array[:, c * grid : (c + 1) * grid]

            l0, m0 = part(lefts, 0), part(mixed, 0)
            terms = [l0 * m0]
            tau = None
            for c in range(1, 4):
                lc, mc = part(lefts, c), part(mixed, c)
                terms.append(lc * m0 + l0 * mc)
                tau = lc * mc if tau is None else tau + lc * mc
            terms.append(tau)
            for q in range(5):
                sums[q] = sums[q] + jnp.sum(terms[q].reshape(chunk // 8, 8, grid), axis=0)
        for q in range(5):
            points[q, pl.ds(b, 1), :] = jnp.sum(sums[q], axis=0, keepdims=True)
        return carry

    lax.fori_loop(0, batches, forward, 0, unroll=True)

    for copy in copies[10:]:
        copy.wait()
    base_rho, base_tau, weights = base_rho_ref[...], base_tau_ref[...], weight_ref[...]

    def energy(grid_rho, grad_x, grad_y, grad_z, grid_tau):
        return point_energy(
            grid_rho, grad_x, grad_y, grad_z, grid_tau, base_rho, base_tau, weights
        )

    values = [points[q] for q in range(5)]
    values[4] = 0.5 * values[4]
    unused, pullback = jax.vjp(energy, *values)
    found = pullback(jnp.ones_like(weights))
    for q in range(5):
        slopes[q] = 0.5 * found[q] if q == 4 else found[q]

    def backward(b, carry):
        mask, take, rows = masks[b].astype(F32), takes[b], batch_rows(b)
        by = [slopes[q, pl.ds(b, 1), :] for q in range(5)]
        right = basis[b].reshape(basis_rows, 4 * grid).astype(F32)
        part = [right[:, c * grid : (c + 1) * grid] for c in range(4)]
        bent = [by[0] * part[0] + by[1] * part[1] + by[2] * part[2] + by[3] * part[3]]
        for c in range(1, 4):
            bent.append(by[c] * part[0] + by[4] * part[c])
        bent = jnp.concatenate([each.astype(BF16) for each in bent], axis=1)
        outer_s[...] = dot_nt(left[b], bent).astype(BF16)
        for m in range(edge):
            own = dot(take, outer_s[m * blocks : (m + 1) * blocks, :]) * mask
            folded = own[:, :LANES]
            for q in range(1, copies_across):
                folded = folded + own[:, q * LANES : (q + 1) * LANES]
            gathered[rows, m * LANES : (m + 1) * LANES] = folded.astype(BF16)
        return carry

    lax.fori_loop(0, batches, backward, 0, unroll=True)
    xc_rows = dot(gathered[...], gather_up[...]).astype(BF16)
    xc_send[...] = dot(drop[:, coul_rows:], xc_rows).astype(BF16)
    push(xc_send, xc_recv, xc_send_sem, xc_recv_sem)
    both_out[0] = total(coul_send, coul_recv, coul_send_sem, coul_recv_sem)
    both_out[1] = total(xc_send, xc_recv, xc_send_sem, xc_recv_sem)


def part_outputs(both_ref, coul_ref, xc_ref, sem):
    copies = [
        pltpu.make_async_copy(both_ref.at[0], coul_ref, sem.at[0]),
        pltpu.make_async_copy(both_ref.at[1], xc_ref, sem.at[1]),
    ]
    for copy in copies:
        copy.start()
    for copy in copies:
        copy.wait()


def body(
    density,
    three_center,
    metric,
    fetch_owner,
    fetch_slot,
    basis_value,
    basis_gradient,
    pair_slot,
    base_density,
    base_kinetic,
    grid_weight,
):
    devices = lax.axis_size("tile")
    tile_count, width = density.shape
    aux, listed = three_center.shape[:2]
    batches, refs = pair_slot.shape[:2]
    blocks, edge, grid = basis_value.shape[1:]
    coul_rows = aux * listed
    total_refs = coul_rows + batches * refs
    sizes = (devices, tile_count, width, aux, listed, batches, refs, blocks, edge, grid)
    vmem = pl.BlockSpec(memory_space=pltpu.VMEM)
    far = pl.BlockSpec(memory_space=pl.ANY)
    total_tiles = devices * tile_count
    basis_rows = blocks * edge
    out = jax.ShapeDtypeStruct((tile_count, width), F32)
    semaphores = pltpu.SemaphoreType.DMA((devices,))
    both = pl.pallas_call(
        functools.partial(kernel, sizes),
        out_shape=jax.ShapeDtypeStruct((2, tile_count, width), F32),
        in_specs=[far] * 11,
        out_specs=vmem,
        scratch_shapes=[
            pltpu.VMEM((1, total_refs), jnp.int32),
            pltpu.VMEM((total_refs,), jnp.int32),
            pltpu.VMEM((batches, 2, refs), jnp.int32),
            pltpu.VMEM((batches, grid), F32),
            pltpu.VMEM((batches, grid), F32),
            pltpu.VMEM((batches, grid), F32),
            pltpu.VMEM(metric.shape, F32),
            pltpu.VMEM((total_tiles, width), BF16),
            pltpu.VMEM(three_center.shape, BF16),
            pltpu.VMEM((batches, blocks, edge, 4 * grid), BF16),
            pltpu.VMEM((batches, basis_rows, 4 * grid), BF16),
            pltpu.VMEM((width, edge * LANES), BF16),
            pltpu.VMEM((edge * LANES, width), BF16),
            pltpu.VMEM((total_refs, total_tiles), BF16),
            pltpu.VMEM((basis_rows, 4 * grid), F32),
            pltpu.VMEM((basis_rows, basis_rows), BF16),
            pltpu.VMEM((batches * refs, edge * LANES), BF16),
            pltpu.VMEM((basis_rows, basis_rows), BF16),
            pltpu.VMEM((basis_rows, basis_rows), BF16),
            pltpu.VMEM((batches, refs, basis_rows), BF16),
            pltpu.VMEM((batches, refs, blocks), BF16),
            pltpu.VMEM((batches * refs, edge * LANES), BF16),
            pltpu.VMEM((coul_rows, width), F32),
            pltpu.VMEM((5, batches, grid), F32),
            pltpu.VMEM((5, batches, grid), F32),
            pltpu.VMEM((total_tiles, width), BF16),
            pltpu.VMEM((total_tiles, width), BF16),
            pltpu.VMEM((devices, tile_count, width), BF16),
            pltpu.VMEM((devices, tile_count, width), BF16),
            pltpu.SemaphoreType.DMA((13,)),
            semaphores,
            semaphores,
            semaphores,
            semaphores,
            semaphores,
            semaphores,
        ],
        compiler_params=pltpu.CompilerParams(
            collective_id=0, has_side_effects=True, vmem_limit_bytes=60 * 1024 * 1024
        ),
        name="fock_build",
    )(
        density,
        metric,
        fetch_owner.reshape(1, total_refs),
        fetch_slot,
        jnp.swapaxes(pair_slot, 1, 2),
        base_density,
        base_kinetic,
        grid_weight,
        three_center,
        basis_value,
        basis_gradient,
    )
    return pl.pallas_call(
        part_outputs,
        out_shape=(out, out),
        in_specs=[far],
        out_specs=(far, far),
        scratch_shapes=[pltpu.SemaphoreType.DMA((2,))],
        name="outputs",
    )(both)


def solution(mesh):
    in_specs = (
        P(("parts", "tile"), None),
        P(("parts", "tile"), None, None, None),
        P(("parts", "tile"), None, None),
        P(("parts", "tile"), None),
        P(("parts", "tile")),
        P(("parts", "tile"), None, None, None),
        P(("parts", "tile"), None, None, None, None),
        P(("parts", "tile"), None, None),
        P(("parts", "tile"), None),
        P(("parts", "tile"), None),
        P(("parts", "tile"), None),
    )
    out_specs = (P(("parts", "tile"), None), P(("parts", "tile"), None))
    return jax.shard_map(body, mesh=mesh, in_specs=in_specs, out_specs=out_specs, check_vma=False)
```
